128 devices in a mesh: depth: 4 (over z_lo, core), inw: 8 (over z_hi, x), outw: 4 (over y).
Axes of the slice: x: 4, y: 4, z: 4 (z_hi: 2, z_lo: 2; z = z_hi * 2 + z_lo), core: 2. Of those that a mesh axis runs over, the one named last changes fastest.
Arguments:
- inputs: bfloat16 [1536, 8192], P(('depth', 'inw'), 'outw'), may hold values from -6 to 6
- w_gate: bfloat16 [8192, 14336], P(('outw', 'depth'), 'inw'), may hold values from -0.0625 to 0.0625
- w_up: bfloat16 [8192, 14336], P(('outw', 'depth'), 'inw'), may hold values from -0.0625 to 0.0625
- w_down: bfloat16 [14336, 8192], P('inw', ('outw', 'depth')), may hold values from -0.046875 to 0.046875
- cotangent: bfloat16 [1536, 8192], P(('depth', 'inw'), 'outw'), may hold values from -1.5 to 1.5
Outputs:
- outputs: bfloat16 [1536, 8192], P(('depth', 'inw'), 'outw')
- grad_inputs: bfloat16 [1536, 8192], P(('depth', 'inw'), 'outw')
- grad_gate: bfloat16 [8192, 14336], P(('outw', 'depth'), 'inw')
- grad_up: bfloat16 [8192, 14336], P(('outw', 'depth'), 'inw')
- grad_down: bfloat16 [14336, 8192], P('inw', ('outw', 'depth'))
The draws below stay inside these ranges and needn't reach their ends.
All inputs are finite; a program needn't handle non-finite values.
Results may differ from the reference program's by a relative error of at most 0.027.
Values may be sent and summed in bfloat16 or wider, within the bound.
No kernel may reach another device: no remote copies, remote signals or barrier semaphores. Data moves between devices by JAX's collectives and lax.ppermute only.
A program may use at most 128 MiB of HBM per device.

```python
import jax
import jax.numpy as jnp
from jax import lax

D = 8192
FF = 14336
TOKENS = 1536
N_DEPTH = 4
N_INW = 8
N_OUTW = 4


def shard_levels(stream_key, extent, pieces, smallest, largest):
    loudness, own = 1.0, jax.random.fold_in(stream_key, 6)
    for dim, blocks in pieces:
        draws = jnp.exp(jax.random.uniform(jax.random.fold_in(own, dim), (blocks,), jnp.float32, smallest / len(pieces), largest / len(pieces)))
        loudness = loudness * jnp.repeat(draws, extent[dim] // blocks).reshape([-1 if axis == dim else 1 for axis in range(len(extent))])
    return loudness


def gaussian(rng, dims, scale, most, shards=(), kind=jnp.bfloat16):
    level = shard_levels(rng, dims, shards, -0.22, 0.18) if shards else 1.0
    array = jax.random.normal(rng, dims, jnp.float32) * scale * level
    return jnp.minimum(jnp.maximum(array, -most), most).astype(kind)


def setup_inputs(seed: int = 0) -> dict:
    seeds = jax.random.split(jax.random.key(seed), 6)
    inputs = gaussian(seeds[0], (TOKENS, D), 1.0, 6.0, ((0, 32), (1, 4)))
    w_gate = gaussian(seeds[1], (D, FF), D ** -0.5, 0.0625, ((0, 16), (1, 8)))
    w_up = gaussian(seeds[2], (D, FF), D ** -0.5, 0.0625, ((0, 16), (1, 8)))
    w_down = gaussian(seeds[3], (FF, D), FF ** -0.5, 0.046875, ((0, 8), (1, 16)))
    cotangent = gaussian(seeds[4], (TOKENS, D), 0.25, 1.5, ((0, 32), (1, 4)))
    return dict(inputs=inputs, w_gate=w_gate, w_up=w_up, w_down=w_down, cotangent=cotangent)


def rounded(value):
    return lax.optimization_barrier(value.astype(jnp.bfloat16)).astype(jnp.float32)


def feature_blocks(left, right, blocks):
    width = left.shape[1] // blocks
    total = jnp.zeros((left.shape[0], right.shape[1]), jnp.float32)
    for block_index in range(blocks):
        lower = block_index * width
        term = jnp.dot(left[:, lower:lower + width], right[lower:lower + width, :], preferred_element_type=jnp.float32)
        total = total + rounded(term)
    return total


def token_blocks(left, right, blocks):
    height = left.shape[0] // blocks
    total = jnp.zeros((left.shape[1], right.shape[1]), jnp.float32)
    for block_index in range(blocks):
        lower = block_index * height
        term = jnp.dot(left[lower:lower + height].T, right[lower:lower + height], preferred_element_type=jnp.float32)
        total = total + rounded(term)
    return total


def reference(inputs, w_gate, w_up, w_down, cotangent):
    gate_sum = feature_blocks(inputs, w_gate, N_OUTW)
    up_sum = feature_blocks(inputs, w_up, N_OUTW)
    hidden = (jax.nn.silu(gate_sum) * up_sum).astype(jnp.bfloat16)
    outputs = feature_blocks(hidden, w_down, N_INW).astype(jnp.bfloat16)
    grad_hidden = feature_blocks(cotangent, w_down.T, N_OUTW)
    sigmoid_gate = jax.nn.sigmoid(gate_sum)
    grad_gate_act = (grad_hidden * up_sum * sigmoid_gate * (1.0 + gate_sum * (1.0 - sigmoid_gate))).astype(jnp.bfloat16)
    grad_up_act = (grad_hidden * gate_sum * sigmoid_gate).astype(jnp.bfloat16)
    width = FF // N_INW
    total = jnp.zeros((inputs.shape[0], D), jnp.float32)
    for block_index in range(N_INW):
        lower = block_index * width
        term = jnp.dot(grad_gate_act[:, lower:lower + width], w_gate[:, lower:lower + width].T, preferred_element_type=jnp.float32)
        term = term + jnp.dot(grad_up_act[:, lower:lower + width], w_up[:, lower:lower + width].T, preferred_element_type=jnp.float32)
        total = total + rounded(term)
    grad_inputs = total.astype(jnp.bfloat16)
    grad_gate = token_blocks(inputs, grad_gate_act, N_DEPTH).astype(jnp.bfloat16)
    grad_up = token_blocks(inputs, grad_up_act, N_DEPTH).astype(jnp.bfloat16)
    grad_down = token_blocks(hidden, cotangent, N_DEPTH).astype(jnp.bfloat16)
    return (outputs, grad_inputs, grad_gate, grad_up, grad_down)
```

```python
import jax
import jax.numpy as jnp
from jax import lax
from jax.sharding import PartitionSpec as P

BF16, F32 = jnp.bfloat16, jnp.float32
STREAMS = 3
ORDERS = (("a", "b", "z"), ("b", "z", "a"), ("z", "a", "b"))


def dot(left, right, dims):
    return lax.dot_general(left, right, (dims, ((), ())), preferred_element_type=F32).astype(BF16)


def swap(value, axis, size, flip):
    return lax.ppermute(value, axis, [(i, i ^ flip) for i in range(size)])


def swap_core(value):
    return swap(value, "depth", 4, 1)


def swap_zlo(value):
    return swap(value, "depth", 4, 2)


def swap_zhi(value):
    return swap(value, "inw", 8, 4)


def swap_zboth(value):
    return lax.ppermute(value, ("depth", "inw"), [(i, i ^ 0b10100) for i in range(32)])


def swap_x(value, flip):
    return swap(value, "inw", 8, flip)


def swap_link(value, link):
    if link == "z":
        return swap_zlo(value)
    return swap(value, "outw", 4, 1 if link == "a" else 3)


def add(*terms):
    total = terms[0].astype(F32)
    for term in terms[1:]:
        total = total + term.astype(F32)
    return total


def either(bit, if_zero, if_one):
    return jnp.where(bit == 0, if_zero, if_one)


def ordered(bit, own, other, axis):
    return either(bit, jnp.concatenate([own, other], axis), jnp.concatenate([other, own], axis))


def half(value, index):
    size = value.shape[0] // 2
    return lax.dynamic_slice_in_dim(value, index * size, size, 0)


def reduce_rows(part, links, bits):
    value = part
    for link in links:
        received = swap_link(half(value, 1 - bits[link]), link)
        value = add(half(value, bits[link]), received)
        if link != links[-1]:
            value = value.astype(BF16)
    return value


def gather_rows(value, links, bits):
    for link in links[::-1]:
        value = ordered(bits[link], value, swap_link(value, link), 0)
    return value


def gather_tokens(local, zlo, core):
    rows = local.reshape(STREAMS, 16, 2048)

    def columns(z, c):
        return lax.dynamic_slice_in_dim(rows, (z * 2 + c) * 512, 512, 2)

    keep = jnp.concatenate([columns(zlo, core), columns(zlo, 1 - core)], 2)
    give = jnp.concatenate([columns(1 - zlo, core), columns(1 - zlo, 1 - core)], 2)
    from_lo, from_hi, from_both = swap_zlo(give), swap_zhi(keep), swap_zboth(give)
    own = jnp.concatenate([ordered(zlo, keep, from_lo, 1), ordered(zlo, from_hi, from_both, 1)], 1)
    first, third = swap_x(own, 1), swap_x(own, 3)
    top, bottom = swap_x(third[:, :32], 1), swap_x(first[:, 32:], 3)
    return jnp.concatenate([own, first, third, top, bottom], 1)


def scatter_tokens(part, zlo, core):
    own, first, third, top, bottom = (
        part[:, 0:64], part[:, 64:128], part[:, 128:192], part[:, 192:224], part[:, 224:256],
    )
    to_third, to_first = swap_x(top, 1), swap_x(bottom, 3)
    first = jnp.concatenate([first[:, :32], add(first[:, 32:], to_first).astype(BF16)], 1)
    third = jnp.concatenate([add(third[:, :32], to_third).astype(BF16), third[:, 32:]], 1)
    own = add(own, swap_x(first, 1), swap_x(third, 3)).astype(BF16)
    near, far = own[:, :32], own[:, 32:]

    def rows_of(value, z):
        return lax.dynamic_slice_in_dim(value, z * 16, 16, 1)

    from_lo = swap_zlo(rows_of(near, 1 - zlo))
    from_hi = swap_zhi(rows_of(far, zlo))
    from_both = swap_zboth(rows_of(far, 1 - zlo))
    mine = add(rows_of(near, zlo), from_hi).astype(BF16)
    other = add(from_lo, from_both).astype(BF16)

    def unswapped(value):
        return ordered(core, value[:, :, :512], value[:, :, 512:], 2)

    out = ordered(zlo, unswapped(mine), unswapped(other), 2)
    return out.reshape(STREAMS * 16, 2048)


def body(inputs, w_gate, w_up, w_down, cotangent):
    depth, outw = lax.axis_index("depth"), lax.axis_index("outw")
    zlo, core = depth >> 1, depth & 1
    bits = {"a": (outw & 1) ^ (outw >> 1), "b": outw >> 1, "z": zlo}

    x_all = gather_tokens(inputs, zlo, core)
    cot_all = gather_tokens(cotangent, zlo, core)
    gate_up = jnp.concatenate(
        [
            jnp.concatenate([w_gate, swap_core(w_gate)], 0),
            jnp.concatenate([w_up, swap_core(w_up)], 0),
        ],
        1,
    )
    down = jnp.concatenate([w_down, swap_core(w_down)], 1)

    sums = [
        reduce_rows(dot(x_all[s], gate_up, ((1,), (0,))), ORDERS[s], bits) for s in range(STREAMS)
    ]
    hidden_grads = [
        reduce_rows(dot(cot_all[s], down, ((1,), (1,))), ORDERS[s], bits) for s in range(STREAMS)
    ]
    hidden, acts = [], []
    for s in range(STREAMS):
        gate_sum, up_sum = sums[s][:, :1792], sums[s][:, 1792:]
        local = (jax.nn.silu(gate_sum) * up_sum).astype(BF16)
        hidden.append(gather_rows(local, ORDERS[s], bits))
    for s in range(STREAMS):
        gate_sum, up_sum = sums[s][:, :1792], sums[s][:, 1792:]
        grad_hidden = hidden_grads[s]
        sigmoid_gate = jax.nn.sigmoid(gate_sum)
        grad_gate_act = (
            grad_hidden * up_sum * sigmoid_gate * (1.0 + gate_sum * (1.0 - sigmoid_gate))
        ).astype(BF16)
        grad_up_act = (grad_hidden * gate_sum * sigmoid_gate).astype(BF16)
        local = jnp.concatenate([grad_gate_act, grad_up_act], 1)
        acts.append(gather_rows(local, ORDERS[s], bits))

    output_part = jnp.stack([dot(h, down, ((1,), (0,))) for h in hidden])
    outputs = scatter_tokens(output_part, zlo, core)
    input_part = jnp.stack([dot(a, gate_up, ((1,), (1,))) for a in acts])
    grad_inputs = scatter_tokens(input_part, zlo, core)

    hidden_all = jnp.concatenate(hidden, 0)
    acts_all = jnp.concatenate(acts, 0)
    x_rows = x_all.reshape(768, 1024)
    cot_rows = cot_all.reshape(768, 1024)
    down_other = swap_core(dot(hidden_all, cot_rows[:, 512:], ((0,), (0,))))
    grad_down = add(dot(hidden_all, cot_rows[:, :512], ((0,), (0,))), down_other).astype(BF16)
    act_other = swap_core(dot(x_rows[:, 512:], acts_all, ((0,), (0,))))
    act_own = dot(x_rows[:, :512], acts_all, ((0,), (0,)))
    grad_gate = add(act_own[:, :1792], act_other[:, :1792]).astype(BF16)
    grad_up = add(act_own[:, 1792:], act_other[:, 1792:]).astype(BF16)
    return outputs, grad_inputs, grad_gate, grad_up, grad_down


def solution(mesh):
    tokens = P(("depth", "inw"), "outw")
    w_in = P(("outw", "depth"), "inw")
    w_out = P("inw", ("outw", "depth"))
    return jax.shard_map(
        body,
        mesh=mesh,
        in_specs=(tokens, w_in, w_in, w_out, tokens),
        out_specs=(tokens, tokens, w_in, w_in, w_out),
        check_vma=False,
    )
```

```python
import jax
import jax.numpy as jnp
from jax import lax
from jax.sharding import PartitionSpec as P

BF16, F32 = jnp.bfloat16, jnp.float32
STREAMS = 3
ORDERS = (("a", "b", "z"), ("b", "z", "a"), ("z", "a", "b"))


def dot(left, right, dims):
    return lax.dot_general(left, right, (dims, ((), ())), preferred_element_type=F32).astype(BF16)


def swap(value, axis, size, flip):
    return lax.ppermute(value, axis, [(i, i ^ flip) for i in range(size)])


def swap_core(value):
    return swap(value, "depth", 4, 1)


def swap_zlo(value):
    return swap(value, "depth", 4, 2)


def swap_zhi(value):
    return swap(value, "inw", 8, 4)


def swap_zboth(value):
    return lax.ppermute(value, ("depth", "inw"), [(i, i ^ 0b10100) for i in range(32)])


def swap_x(value, flip):
    return swap(value, "inw", 8, flip)


def swap_link(value, link):
    if link == "z":
        return swap_zlo(value)
    return swap(value, "outw", 4, 1 if link == "a" else 3)


def add(*terms):
    total = terms[0].astype(F32)
    for term in terms[1:]:
        total = total + term.astype(F32)
    return total


def either(bit, if_zero, if_one):
    return jnp.where(bit == 0, if_zero, if_one)


def ordered(bit, own, other, axis):
    return either(bit, jnp.concatenate([own, other], axis), jnp.concatenate([other, own], axis))


def half(value, index):
    size = value.shape[0] // 2
    return lax.dynamic_slice_in_dim(value, index * size, size, 0)


def together(*values):
    return lax.optimization_barrier(values)


def after(value, *others):
    marks = [
        lax.slice(array, [0] * array.ndim, [1] * array.ndim)
        for array in jax.tree.leaves(lax.optimization_barrier(others))
    ]
    return lax.optimization_barrier((value, marks))[0]


def reduce_give(parts, link, bits):
    return jnp.stack([half(part, 1 - bits[link]) for part in parts])


def reduce_take(parts, received, link, bits):
    return [add(half(part, bits[link]), received[i]) for i, part in enumerate(parts)]


def rounded(parts):
    return [part.astype(BF16) for part in parts]


def doubled(value, received, link, bits):
    return ordered(bits[link], value, received, 1)


def near_gives(local, zlo, core):
    rows = local.reshape(STREAMS, 16, 2048)

    def columns(z, c):
        return lax.dynamic_slice_in_dim(rows, (z * 2 + c) * 512, 512, 2)

    keep = jnp.concatenate([columns(zlo, core), columns(zlo, 1 - core)], 2)
    give = jnp.concatenate([columns(1 - zlo, core), columns(1 - zlo, 1 - core)], 2)
    return together(keep, give)


def near_send(keep, give):
    return together(swap_zlo(give), swap_zhi(keep), swap_zboth(give))


def near_gathered(keep, received, zlo):
    from_lo, from_hi, from_both = received
    return jnp.concatenate([ordered(zlo, keep, from_lo, 1), ordered(zlo, from_hi, from_both, 1)], 1)


def x_send(to_first, to_third):
    return together(swap_x(to_first, 1), swap_x(to_third, 3))


def relays(first, third):
    return together(third[:, :32], first[:, 32:])


def scatter_relays(part, received):
    to_third, to_first = received
    first = jnp.concatenate([part[:, 64:96], add(part[:, 96:128], to_first).astype(BF16)], 1)
    third = jnp.concatenate([add(part[:, 128:160], to_third).astype(BF16), part[:, 160:192]], 1)
    return together(first, third)


def scatter_near(own, zlo):
    near, far = own[:, :32], own[:, 32:]

    def rows_of(value, z):
        return lax.dynamic_slice_in_dim(value, z * 16, 16, 1)

    return rows_of(near, zlo), together(rows_of(near, 1 - zlo), rows_of(far, zlo), rows_of(far, 1 - zlo))


def scatter_send(to_lo, to_hi, to_both):
    return together(swap_zlo(to_lo), swap_zhi(to_hi), swap_zboth(to_both))


def scattered(mine, got, zlo, core):
    from_lo, from_hi, from_both = got
    mine = add(mine, from_hi).astype(BF16)
    other = add(from_lo, from_both).astype(BF16)

    def unswapped(value):
        return ordered(core, value[:, :, :512], value[:, :, 512:], 2)

    return ordered(zlo, unswapped(mine), unswapped(other), 2).reshape(-1, 2048)


def act_grads(grad_hidden, gate_sum, up_sum):
    sigmoid_gate = jax.nn.sigmoid(gate_sum)
    grad_gate_act = (
        grad_hidden * up_sum * sigmoid_gate * (1.0 + gate_sum * (1.0 - sigmoid_gate))
    ).astype(BF16)
    grad_up_act = (grad_hidden * gate_sum * sigmoid_gate).astype(BF16)
    return jnp.stack([grad_gate_act, grad_up_act])


def body(inputs, w_gate, w_up, w_down, cotangent):
    depth, outw = lax.axis_index("depth"), lax.axis_index("outw")
    zlo, core = depth >> 1, depth & 1
    bits = {"a": (outw & 1) ^ (outw >> 1), "b": outw >> 1, "z": zlo}
    streams = range(STREAMS)

    x_keep, x_give = near_gives(inputs, zlo, core)
    gate_got, up_got, x_got, cot = together(
        swap_core(w_gate), swap_core(w_up), near_send(x_keep, x_give), cotangent
    )
    x_near = near_gathered(x_keep, x_got, zlo)
    cot_keep, cot_give = near_gives(cot, zlo, core)
    x_first, cot_got, gate, up = together(
        x_send(x_near, x_near),
        near_send(cot_keep, cot_give),
        jnp.concatenate([w_gate, gate_got], 0),
        jnp.concatenate([w_up, up_got], 0),
    )
    x_second, cot_near, down_got = together(
        x_send(*relays(*x_first)), near_gathered(cot_keep, cot_got, zlo), swap_core(w_down)
    )
    x_all = jnp.concatenate([x_near, *x_first, *x_second], 1)

    s_parts = [[dot(x_all[s], gate, ((1,), (0,))), dot(x_all[s], up, ((1,), (0,)))] for s in streams]
    s_gives = [reduce_give(s_parts[s], ORDERS[s][0], bits) for s in streams]
    cot_first = x_send(cot_near, cot_near)
    cot_first, down = together(after(cot_first, s_gives), jnp.concatenate([w_down, down_got], 1))
    cot_all = jnp.concatenate([cot_near, *cot_first, *x_send(*relays(*cot_first))], 1)
    g_parts = [[dot(cot_all[s], down, ((1,), (1,)))] for s in streams]

    hidden, acts, act_gots = [], [], []
    for s in streams:
        links = ORDERS[s]
        s_part, g_part, s_give = s_parts[s], g_parts[s], s_gives[s]
        g_give = reduce_give(g_part, links[0], bits)
        s_part = rounded(reduce_take(s_part, swap_link(s_give, links[0]), links[0], bits))
        s_give = reduce_give(s_part, links[1], bits)
        g_got = after(swap_link(g_give, links[0]), s_give)
        g_part = rounded(reduce_take(g_part, g_got, links[0], bits))
        g_give = reduce_give(g_part, links[1], bits)
        s_got = after(swap_link(s_give, links[1]), g_give)
        s_part = jnp.stack(rounded(reduce_take(s_part, s_got, links[1], bits)))
        g_got = after(swap_link(g_give, links[1]), s_part)
        g_part = rounded(reduce_take(g_part, g_got, links[1], bits))[0]
        gate_sum, up_sum = add(s_part, after(swap_link(s_part, links[2]), g_part))
        hid = (jax.nn.silu(gate_sum) * up_sum).astype(BF16)[None]
        grad_hidden = add(g_part, after(swap_link(g_part, links[2]), hid))
        act = act_grads(grad_hidden, gate_sum, up_sum)
        hid = doubled(hid, after(swap_link(hid, links[1]), act), links[1], bits)
        act = doubled(act, after(swap_link(act, links[1]), hid), links[1], bits)
        hidden.append(doubled(hid, after(swap_link(hid, links[0]), act), links[0], bits)[0])
        acts.append(act)
        act_gots.append(swap_link(act, links[0]))
    out_part = jnp.stack([dot(h, down, ((1,), (0,))) for h in hidden])
    hidden_all = jnp.concatenate(hidden, 0)
    cot_rows = cot_all.reshape(768, 1024)
    down_other = dot(hidden_all, cot_rows[:, 512:], ((0,), (0,)))
    act_gots, out_got, down_other = together(
        act_gots, x_send(out_part[:, 192:224], out_part[:, 224:256]), down_other
    )

    acts = [doubled(acts[s], act_gots[s], ORDERS[s][0], bits) for s in streams]

    def input_term(act):
        left = lax.dot_general(act[0], gate, (((1,), (1,)), ((), ())), preferred_element_type=F32)
        right = lax.dot_general(act[1], up, (((1,), (1,)), ((), ())), preferred_element_type=F32)
        return (left + right).astype(BF16)

    def own_plus(left, right, got):
        return add(lax.dot_general(left, right, (((0,), (0,)), ((), ())), preferred_element_type=F32), got).astype(BF16)

    in_part = jnp.stack([input_term(act) for act in acts])
    out_relays = scatter_relays(out_part, out_got)
    x_rows = x_all.reshape(768, 1024)
    act_gate = jnp.concatenate([act[0] for act in acts], 0)
    act_up = jnp.concatenate([act[1] for act in acts], 0)
    gate_other = dot(x_rows[:, 512:], act_gate, ((0,), (0,)))
    in_got, out_got, down_got, gate_other = together(
        x_send(in_part[:, 192:224], in_part[:, 224:256]),
        x_send(*out_relays),
        swap_core(down_other),
        gate_other,
    )
    in_relays = scatter_relays(in_part, in_got)
    up_other = dot(x_rows[:, 512:], act_up, ((0,), (0,)))
    in_got, gate_got, up_got, grad_down, out_own = together(
        x_send(*in_relays),
        swap_core(gate_other),
        swap_core(up_other),
        own_plus(hidden_all, cot_rows[:, :512], down_got),
        add(out_part[:, :64], *out_got).astype(BF16),
    )
    in_own = add(in_part[:, :64], *in_got).astype(BF16)
    mine, gives = scatter_near(jnp.concatenate([out_own, in_own], 0), zlo)
    got, grad_gate, grad_up = together(
        scatter_send(*gives),
        own_plus(x_rows[:, :512], act_gate, gate_got),
        own_plus(x_rows[:, :512], act_up, up_got),
    )
    both = scattered(mine, got, zlo, core)
    return both[:48], both[48:], grad_gate, grad_up, grad_down


def solution(mesh):
    tokens = P(("depth", "inw"), "outw")
    w_in = P(("outw", "depth"), "inw")
    w_out = P("inw", ("outw", "depth"))
    return jax.shard_map(
        body,
        mesh=mesh,
        in_specs=(tokens, w_in, w_in, w_out, tokens),
        out_specs=(tokens, tokens, w_in, w_in, w_out),
        check_vma=False,
    )
```

```python
import jax
import jax.numpy as jnp
from jax import lax
from jax.sharding import PartitionSpec as P

BF16, F32 = jnp.bfloat16, jnp.float32
STREAMS = 3
ORDERS = (("a", "b", "z"), ("b", "z", "a"), ("z", "a", "b"))


def dot(left, right, dims):
    return lax.dot_general(left, right, (dims, ((), ())), preferred_element_type=F32).astype(BF16)


def swap(value, axis, size, flip):
    return lax.ppermute(value, axis, [(i, i ^ flip) for i in range(size)])


def swap_core(value):
    return swap(value, "depth", 4, 1)


def swap_zlo(value):
    return swap(value, "depth", 4, 2)


def swap_zhi(value):
    return swap(value, "inw", 8, 4)


def swap_zboth(value):
    return lax.ppermute(value, ("depth", "inw"), [(i, i ^ 0b10100) for i in range(32)])


def swap_x(value, flip):
    return swap(value, "inw", 8, flip)


def swap_link(value, link):
    if link == "z":
        return swap_zlo(value)
    return swap(value, "outw", 4, 1 if link == "a" else 3)


def add(*terms):
    total = terms[0].astype(F32)
    for term in terms[1:]:
        total = total + term.astype(F32)
    return total


def either(bit, if_zero, if_one):
    return jnp.where(bit == 0, if_zero, if_one)


def ordered(bit, own, other, axis):
    return either(bit, jnp.concatenate([own, other], axis), jnp.concatenate([other, own], axis))


def half(value, index):
    size = value.shape[0] // 2
    return lax.dynamic_slice_in_dim(value, index * size, size, 0)


def together(*values):
    return lax.optimization_barrier(values)


def after(value, *others):
    marks = [
        lax.slice(array, [0] * array.ndim, [1] * array.ndim)
        for array in jax.tree.leaves(lax.optimization_barrier(others))
    ]
    return lax.optimization_barrier((value, marks))[0]


def reduce_give(parts, link, bits):
    return jnp.stack([half(part, 1 - bits[link]) for part in parts])


def reduce_take(parts, received, link, bits):
    return [add(half(part, bits[link]), received[i]) for i, part in enumerate(parts)]


def rounded(parts):
    return [part.astype(BF16) for part in parts]


def doubled(value, received, link, bits):
    return ordered(bits[link], value, received, 1)


def near_gives(local, zlo, core):
    rows = local.reshape(STREAMS, 16, 2048)

    def columns(z, c):
        return lax.dynamic_slice_in_dim(rows, (z * 2 + c) * 512, 512, 2)

    keep = jnp.concatenate([columns(zlo, core), columns(zlo, 1 - core)], 2)
    give = jnp.concatenate([columns(1 - zlo, core), columns(1 - zlo, 1 - core)], 2)
    return together(keep, give)


def near_send(keep, give):
    return together(swap_zlo(give), swap_zhi(keep), swap_zboth(give))


def near_gathered(keep, received, zlo):
    from_lo, from_hi, from_both = received
    return jnp.concatenate([ordered(zlo, keep, from_lo, 1), ordered(zlo, from_hi, from_both, 1)], 1)


def x_send(to_first, to_third):
    return together(swap_x(to_first, 1), swap_x(to_third, 3))


def relays(first, third):
    return together(third[:, :32], first[:, 32:])


def scatter_relays(part, received):
    to_third, to_first = received
    first = jnp.concatenate([part[:, 64:96], add(part[:, 96:128], to_first).astype(BF16)], 1)
    third = jnp.concatenate([add(part[:, 128:160], to_third).astype(BF16), part[:, 160:192]], 1)
    return together(first, third)


def scatter_near(own, zlo):
    near, far = own[:, :32], own[:, 32:]

    def rows_of(value, z):
        return lax.dynamic_slice_in_dim(value, z * 16, 16, 1)

    return rows_of(near, zlo), together(rows_of(near, 1 - zlo), rows_of(far, zlo), rows_of(far, 1 - zlo))


def scatter_send(to_lo, to_hi, to_both):
    return together(swap_zlo(to_lo), swap_zhi(to_hi), swap_zboth(to_both))


def scattered(mine, got, zlo, core):
    from_lo, from_hi, from_both = got
    mine = add(mine, from_hi).astype(BF16)
    other = add(from_lo, from_both).astype(BF16)

    def unswapped(value):
        return ordered(core, value[:, :, :512], value[:, :, 512:], 2)

    return ordered(zlo, unswapped(mine), unswapped(other), 2).reshape(-1, 2048)


def act_grads(grad_hidden, gate_sum, up_sum):
    sigmoid_gate = jax.nn.sigmoid(gate_sum)
    grad_gate_act = (
        grad_hidden * up_sum * sigmoid_gate * (1.0 + gate_sum * (1.0 - sigmoid_gate))
    ).astype(BF16)
    grad_up_act = (grad_hidden * gate_sum * sigmoid_gate).astype(BF16)
    return jnp.stack([grad_gate_act, grad_up_act])


def body(inputs, w_gate, w_up, w_down, cotangent):
    depth, outw = lax.axis_index("depth"), lax.axis_index("outw")
    zlo, core = depth >> 1, depth & 1
    bits = {"a": (outw & 1) ^ (outw >> 1), "b": outw >> 1, "z": zlo}
    streams = range(STREAMS)

    x_keep, x_give = near_gives(inputs, zlo, core)
    gate_got, up_got, x_got, cot = together(
        swap_core(w_gate), swap_core(w_up), near_send(x_keep, x_give), cotangent
    )
    x_near = near_gathered(x_keep, x_got, zlo)
    cot_keep, cot_give = near_gives(cot, zlo, core)
    x_first, cot_got, gate, up = together(
        x_send(x_near, x_near),
        near_send(cot_keep, cot_give),
        jnp.concatenate([w_gate, gate_got], 0),
        jnp.concatenate([w_up, up_got], 0),
    )
    x_second, cot_near, down_got = together(
        x_send(*relays(*x_first)), near_gathered(cot_keep, cot_got, zlo), swap_core(w_down)
    )
    x_all = jnp.concatenate([x_near, *x_first, *x_second], 1)

    s_parts = [[dot(x_all[s], gate, ((1,), (0,))), dot(x_all[s], up, ((1,), (0,)))] for s in streams]
    s_gives = [reduce_give(s_parts[s], ORDERS[s][0], bits) for s in streams]
    cot_first = x_send(cot_near, cot_near)
    cot_first, down = together(after(cot_first, s_gives), jnp.concatenate([w_down, down_got], 1))
    cot_all = jnp.concatenate([cot_near, *cot_first, *x_send(*relays(*cot_first))], 1)
    g_parts = [[dot(cot_all[s], down, ((1,), (1,)))] for s in streams]

    hidden, acts, act_gots = [], [], []
    for s in streams:
        links = ORDERS[s]
        s_part, g_part, s_give = s_parts[s], g_parts[s], s_gives[s]
        g_give = reduce_give(g_part, links[0], bits)
        s_part = rounded(reduce_take(s_part, swap_link(s_give, links[0]), links[0], bits))
        s_give = reduce_give(s_part, links[1], bits)
        g_got, s_part = together(swap_link(g_give, links[0]), s_part)
        g_part = rounded(reduce_take(g_part, g_got, links[0], bits))
        g_give = reduce_give(g_part, links[1], bits)
        s_got, g_part = together(swap_link(s_give, links[1]), g_part)
        s_give = jnp.stack(rounded(reduce_take(s_part, s_got, links[1], bits)))
        g_got, s_part = together(swap_link(g_give, links[1]), s_give)
        g_give = rounded(reduce_take(g_part, g_got, links[1], bits))[0]
        s_got, g_part = together(swap_link(s_give, links[2]), g_give)
        gate_sum, up_sum = add(s_part, s_got)
        hid = (jax.nn.silu(gate_sum) * up_sum).astype(BF16)[None]
        grad_hidden = add(g_part, after(swap_link(g_give, links[2]), hid))
        act = act_grads(grad_hidden, gate_sum, up_sum)
        hid = doubled(hid, swap_link(hid, links[1]), links[1], bits)
        act = doubled(act, swap_link(act, links[1]), links[1], bits)
        hidden.append(doubled(hid, swap_link(hid, links[0]), links[0], bits)[0])
        acts.append(act)
        act_gots.append(swap_link(act, links[0]))
    out_part = jnp.stack([dot(h, down, ((1,), (0,))) for h in hidden])
    hidden_all = jnp.concatenate(hidden, 0)
    cot_rows = cot_all.reshape(768, 1024)
    down_other = dot(hidden_all, cot_rows[:, 512:], ((0,), (0,)))
    act_gots, out_got, down_other = together(
        act_gots, x_send(out_part[:, 192:224], out_part[:, 224:256]), down_other
    )

    acts = [doubled(acts[s], act_gots[s], ORDERS[s][0], bits) for s in streams]

    def input_term(act):
        left = lax.dot_general(act[0], gate, (((1,), (1,)), ((), ())), preferred_element_type=F32)
        right = lax.dot_general(act[1], up, (((1,), (1,)), ((), ())), preferred_element_type=F32)
        return (left + right).astype(BF16)

    def own_plus(left, right, got):
        return add(lax.dot_general(left, right, (((0,), (0,)), ((), ())), preferred_element_type=F32), got).astype(BF16)

    in_part = jnp.stack([input_term(act) for act in acts])
    in_second = in_part[:, 192:]
    out_relays = scatter_relays(out_part, out_got)
    x_rows = x_all.reshape(768, 1024)
    act_gate = jnp.concatenate([act[0] for act in acts], 0)
    act_up = jnp.concatenate([act[1] for act in acts], 0)
    gate_other = dot(x_rows[:, 512:], act_gate, ((0,), (0,)))
    out_got = x_send(*out_relays)
    in_got, out_got, down_got, gate_other = together(
        x_send(in_second[:, :32], in_second[:, 32:]), out_got, swap_core(down_other), gate_other
    )
    in_relays = scatter_relays(in_part, in_got)
    up_other = dot(x_rows[:, 512:], act_up, ((0,), (0,)))
    out_mine, out_gives = scatter_near(add(out_part[:, :64], *out_got).astype(BF16), zlo)
    out_got = scatter_send(*out_gives)
    gate_got, up_got = swap_core(gate_other), swap_core(up_other)
    grad_down = own_plus(hidden_all, cot_rows[:, :512], down_got)
    in_got, gate_got, up_got, grad_down, out_got = together(
        x_send(*in_relays), gate_got, up_got, grad_down, out_got
    )
    in_mine, in_gives = scatter_near(add(in_part[:, :64], *in_got).astype(BF16), zlo)
    in_got, grad_gate, grad_up, outputs = together(
        scatter_send(*in_gives),
        own_plus(x_rows[:, :512], act_gate, gate_got),
        own_plus(x_rows[:, :512], act_up, up_got),
        scattered(out_mine, out_got, zlo, core),
    )
    grad_inputs = scattered(in_mine, in_got, zlo, core)
    return outputs, grad_inputs, grad_gate, grad_up, grad_down


def solution(mesh):
    tokens = P(("depth", "inw"), "outw")
    w_in = P(("outw", "depth"), "inw")
    w_out = P("inw", ("outw", "depth"))
    return jax.shard_map(
        body,
        mesh=mesh,
        in_specs=(tokens, w_in, w_in, w_out, tokens),
        out_specs=(tokens, tokens, w_in, w_in, w_out),
        check_vma=False,
    )
```

```python
import jax
import jax.numpy as jnp
from jax import lax
from jax.sharding import PartitionSpec as P

BF16, F32 = jnp.bfloat16, jnp.float32
STREAMS = 3
ORDERS = (("a", "b", "z"), ("b", "z", "a"), ("z", "a", "b"))


def dot(left, right, dims):
    return lax.dot_general(left, right, (dims, ((), ())), preferred_element_type=F32).astype(BF16)


def swap(value, axis, size, flip):
    return lax.ppermute(value, axis, [(i, i ^ flip) for i in range(size)])


def swap_core(value):
    return swap(value, "depth", 4, 1)


def swap_zlo(value):
    return swap(value, "depth", 4, 2)


def swap_zhi(value):
    return swap(value, "inw", 8, 4)


def swap_zboth(value):
    return lax.ppermute(value, ("depth", "inw"), [(i, i ^ 0b10100) for i in range(32)])


def swap_x(value, flip):
    return swap(value, "inw", 8, flip)


def swap_link(value, link):
    if link == "z":
        return swap_zlo(value)
    return swap(value, "outw", 4, 1 if link == "a" else 3)


def add(*terms):
    total = terms[0].astype(F32)
    for term in terms[1:]:
        total = total + term.astype(F32)
    return total


def either(bit, if_zero, if_one):
    return jnp.where(bit == 0, if_zero, if_one)


def ordered(bit, own, other, axis):
    return either(bit, jnp.concatenate([own, other], axis), jnp.concatenate([other, own], axis))


def half(value, index):
    size = value.shape[0] // 2
    return lax.dynamic_slice_in_dim(value, index * size, size, 0)


def together(*values):
    return lax.optimization_barrier(values)


def after(value, *others):
    marks = [
        lax.slice(array, [0] * array.ndim, [1] * array.ndim)
        for array in jax.tree.leaves(lax.optimization_barrier(others))
    ]
    return lax.optimization_barrier((value, marks))[0]


def reduce_give(parts, link, bits):
    return jnp.stack([half(part, 1 - bits[link]) for part in parts])


def reduce_take(parts, received, link, bits):
    return [add(half(part, bits[link]), received[i]) for i, part in enumerate(parts)]


def rounded(parts):
    return [part.astype(BF16) for part in parts]


def doubled(value, received, link, bits):
    return ordered(bits[link], value, received, 1)


def near_gives(local, zlo, core):
    rows = local.reshape(STREAMS, 16, 2048)

    def columns(z, c):
        return lax.dynamic_slice_in_dim(rows, (z * 2 + c) * 512, 512, 2)

    keep = jnp.concatenate([columns(zlo, core), columns(zlo, 1 - core)], 2)
    give = jnp.concatenate([columns(1 - zlo, core), columns(1 - zlo, 1 - core)], 2)
    return together(keep, give)


def near_send(keep, give):
    return together(swap_zlo(give), swap_zhi(keep), swap_zboth(give))


def near_gathered(keep, received, zlo):
    from_lo, from_hi, from_both = received
    return jnp.concatenate([ordered(zlo, keep, from_lo, 1), ordered(zlo, from_hi, from_both, 1)], 1)


def x_send(to_first, to_third):
    return together(swap_x(to_first, 1), swap_x(to_third, 3))


def relays(first, third):
    return together(third[:, :32], first[:, 32:])


def scatter_relays(part, received):
    to_third, to_first = received
    first = jnp.concatenate([part[:, 64:96], add(part[:, 96:128], to_first).astype(BF16)], 1)
    third = jnp.concatenate([add(part[:, 128:160], to_third).astype(BF16), part[:, 160:192]], 1)
    return together(first, third)


def scatter_near(own, zlo):
    near, far = own[:, :32], own[:, 32:]

    def rows_of(value, z):
        return lax.dynamic_slice_in_dim(value, z * 16, 16, 1)

    return rows_of(near, zlo), together(rows_of(near, 1 - zlo), rows_of(far, zlo), rows_of(far, 1 - zlo))


def scatter_send(to_lo, to_hi, to_both):
    return together(swap_zlo(to_lo), swap_zhi(to_hi), swap_zboth(to_both))


def scattered(mine, got, zlo, core):
    from_lo, from_hi, from_both = got
    mine = add(mine, from_hi).astype(BF16)
    other = add(from_lo, from_both).astype(BF16)

    def unswapped(value):
        return ordered(core, value[:, :, :512], value[:, :, 512:], 2)

    return ordered(zlo, unswapped(mine), unswapped(other), 2).reshape(-1, 2048)


def act_grads(grad_hidden, gate_sum, up_sum):
    sigmoid_gate = jax.nn.sigmoid(gate_sum)
    grad_gate_act = (
        grad_hidden * up_sum * sigmoid_gate * (1.0 + gate_sum * (1.0 - sigmoid_gate))
    ).astype(BF16)
    grad_up_act = (grad_hidden * gate_sum * sigmoid_gate).astype(BF16)
    return jnp.stack([grad_gate_act, grad_up_act])


def body(inputs, w_gate, w_up, w_down, cotangent):
    depth, outw = lax.axis_index("depth"), lax.axis_index("outw")
    zlo, core = depth >> 1, depth & 1
    bits = {"a": (outw & 1) ^ (outw >> 1), "b": outw >> 1, "z": zlo}
    streams = range(STREAMS)

    x_keep, x_give = near_gives(inputs, zlo, core)
    gate_got, up_got, x_got, cot = together(
        swap_core(w_gate), swap_core(w_up), near_send(x_keep, x_give), cotangent
    )
    x_near = near_gathered(x_keep, x_got, zlo)
    cot_keep, cot_give = near_gives(cot, zlo, core)
    x_first, cot_got, gate, up = together(
        x_send(x_near, x_near),
        near_send(cot_keep, cot_give),
        jnp.concatenate([w_gate, gate_got], 0),
        jnp.concatenate([w_up, up_got], 0),
    )
    x_second, cot_near, down_got = together(
        x_send(*relays(*x_first)), near_gathered(cot_keep, cot_got, zlo), swap_core(w_down)
    )
    x_all = jnp.concatenate([x_near, *x_first, *x_second], 1)

    s_parts = [[dot(x_all[s], gate, ((1,), (0,))), dot(x_all[s], up, ((1,), (0,)))] for s in streams]
    s_gives = [reduce_give(s_parts[s], ORDERS[s][0], bits) for s in streams]
    cot_first = x_send(cot_near, cot_near)
    cot_first, down = together(after(cot_first, s_gives), jnp.concatenate([w_down, down_got], 1))
    cot_all = jnp.concatenate([cot_near, *cot_first, *x_send(*relays(*cot_first))], 1)
    g_parts = [[dot(cot_all[s], down, ((1,), (1,)))] for s in streams]

    hidden, acts, act_gots = [], [], []
    for s in streams:
        links = ORDERS[s]
        s_part, g_part, s_give = s_parts[s], g_parts[s], s_gives[s]
        g_give = reduce_give(g_part, links[0], bits)
        s_part = rounded(reduce_take(s_part, swap_link(s_give, links[0]), links[0], bits))
        s_give = reduce_give(s_part, links[1], bits)
        g_got, s_part = together(swap_link(g_give, links[0]), s_part)
        g_part = rounded(reduce_take(g_part, g_got, links[0], bits))
        g_give = reduce_give(g_part, links[1], bits)
        s_got, g_part = together(swap_link(s_give, links[1]), g_part)
        s_give = jnp.stack(rounded(reduce_take(s_part, s_got, links[1], bits)))
        g_got, s_part = together(swap_link(g_give, links[1]), s_give)
        g_give = rounded(reduce_take(g_part, g_got, links[1], bits))[0]
        s_got, g_part = together(swap_link(s_give, links[2]), g_give)
        gate_sum, up_sum = add(s_part, s_got)
        hid = (jax.nn.silu(gate_sum) * up_sum).astype(BF16)[None]
        grad_hidden = add(g_part, after(swap_link(g_give, links[2]), hid))
        act = act_grads(grad_hidden, gate_sum, up_sum)
        both = jnp.concatenate([hid, act], 0)
        both = doubled(both, swap_link(both, links[1]), links[1], bits)
        hid, act = both[:1], both[1:]
        hidden.append(doubled(hid, swap_link(hid, links[0]), links[0], bits)[0])
        acts.append(act)
        act_gots.append(swap_link(act, links[0]))
    out_part = jnp.stack([dot(h, down, ((1,), (0,))) for h in hidden])
    hidden_all = jnp.concatenate(hidden, 0)
    cot_rows = cot_all.reshape(768, 1024)
    down_other = dot(hidden_all, cot_rows[:, 512:], ((0,), (0,)))
    act_gots, out_got, down_other = together(
        act_gots, x_send(out_part[:, 192:224], out_part[:, 224:256]), down_other
    )

    acts = [doubled(acts[s], act_gots[s], ORDERS[s][0], bits) for s in streams]

    def input_term(act):
        left = lax.dot_general(act[0], gate, (((1,), (1,)), ((), ())), preferred_element_type=F32)
        right = lax.dot_general(act[1], up, (((1,), (1,)), ((), ())), preferred_element_type=F32)
        return (left + right).astype(BF16)

    def own_plus(left, right, got):
        return add(lax.dot_general(left, right, (((0,), (0,)), ((), ())), preferred_element_type=F32), got).astype(BF16)

    in_part = jnp.stack([input_term(act) for act in acts])
    in_second = in_part[:, 192:]
    out_relays = scatter_relays(out_part, out_got)
    x_rows = x_all.reshape(768, 1024)
    act_gate = jnp.concatenate([act[0] for act in acts], 0)
    act_up = jnp.concatenate([act[1] for act in acts], 0)
    gate_other = dot(x_rows[:, 512:], act_gate, ((0,), (0,)))
    out_got = x_send(*out_relays)
    in_got, out_got, down_got, gate_other = together(
        x_send(in_second[:, :32], in_second[:, 32:]), out_got, swap_core(down_other), gate_other
    )
    in_relays = scatter_relays(in_part, in_got)
    up_other = dot(x_rows[:, 512:], act_up, ((0,), (0,)))
    out_mine, out_gives = scatter_near(add(out_part[:, :64], *out_got).astype(BF16), zlo)
    out_got = scatter_send(*out_gives)
    gate_got, up_got = swap_core(gate_other), swap_core(up_other)
    grad_down = own_plus(hidden_all, cot_rows[:, :512], down_got)
    in_got, gate_got, up_got, grad_down, out_got = together(
        x_send(*in_relays), gate_got, up_got, grad_down, out_got
    )
    in_mine, in_gives = scatter_near(add(in_part[:, :64], *in_got).astype(BF16), zlo)
    in_got, grad_gate, grad_up, outputs = together(
        scatter_send(*in_gives),
        own_plus(x_rows[:, :512], act_gate, gate_got),
        own_plus(x_rows[:, :512], act_up, up_got),
        scattered(out_mine, out_got, zlo, core),
    )
    grad_inputs = scattered(in_mine, in_got, zlo, core)
    return outputs, grad_inputs, grad_gate, grad_up, grad_down


def solution(mesh):
    tokens = P(("depth", "inw"), "outw")
    w_in = P(("outw", "depth"), "inw")
    w_out = P("inw", ("outw", "depth"))
    return jax.shard_map(
        body,
        mesh=mesh,
        in_specs=(tokens, w_in, w_in, w_out, tokens),
        out_specs=(tokens, tokens, w_in, w_in, w_out),
        check_vma=False,
    )
```
